256 devices in a mesh: dom: 32 (over y, x, core), blk: 8 (over z).
Axes of the slice: x: 4, y: 4, z: 8, core: 2. Of those that a mesh axis runs over, the one named last changes fastest.
Arguments:
- source: bfloat16 [4096, 192], P(('dom', 'blk')), may hold values from -6 to 6
- lam_init: bfloat16 [4096, 192], P(('dom', 'blk')), may hold values from -6 to 6
- offd: bfloat16 [4096, 192, 1152], P(('dom', 'blk')), may hold values from -0.1875 to 0.1875
- dinv: bfloat16 [192, 786432], P(None, ('dom', 'blk')), may hold values from -0.4375 to 0.4375
- colidx: int32 [4096, 6], P(('dom', 'blk')), may hold values from 0 to 191
- face_list: int32 [32, 64], P('dom'), may hold values from 0 to 127
- partner: int32 [32], P('dom'), may hold values from 0 to 31, as said below
- perf_block: int32 [32768], P(('dom', 'blk')), may hold values from 0 to 15
- perf_well: int32 [32768], P(('dom', 'blk')), may hold values from 0 to 63
- perf_sens: bfloat16 [32768, 192], P(('dom', 'blk')), may hold values from -0.21875 to 0.21875
- obj_weight: float32 [1024], replicated, may hold values from 0.5 to 2
- step_index: int32 [1], replicated, may hold values from 0 to 1023
Outputs:
- adjoint: float32 [4096, 192], P(('dom', 'blk'))
- control_grad: float32 [2048], P(('dom', 'blk'))
The draws below stay inside these ranges and needn't reach their ends.
Inputs may be any that keep to these rules, and one draw needn't show every extreme that they name: Below 128 an own block of the partition, from 128 on halo block colidx - 128. `face_list`: blocks of the partition's own 128, repeats possible. A pairing: partner[p] != p and partner[partner[p]] == p.
All inputs are finite; a program needn't handle non-finite values.
Results may differ from the reference program's by a relative error of at most 0.0054.
Values may be sent and summed in bfloat16 or wider, within the bound.
No kernel may reach another device: no remote copies, remote signals or barrier semaphores. Data moves between devices by JAX's collectives and lax.ppermute only.
A program may use at most 64 MiB of HBM per device.

```python
import math
import jax
import jax.numpy as jnp
import numpy as np
from jax import lax

BW = 192
K = 6
BD = 16
PD = 128
WP = 64
CK = 1024
PARTS_SIZE = 32
PB = 128
FB = 64
TOTAL_BLOCKS = 4096
TOTAL_PERF = 32768
N_BLK = 8


def draw_partner(key, part):
    key = jax.random.fold_in(key, 11)
    half_count = PARTS_SIZE // 2
    first_key, second_key = jax.random.split(key)
    anchor = jax.random.randint(first_key, (), 0, half_count).astype(jnp.int32)
    ranks = jax.random.permutation(second_key, PARTS_SIZE).astype(jnp.int32)
    indices = jnp.arange(PARTS_SIZE, dtype=jnp.int32)
    lifted = jnp.where((indices == anchor) | (indices == anchor + half_count), PARTS_SIZE + indices, ranks)
    order = jnp.argsort(lifted, stable=True).astype(jnp.int32)
    firsts = order[0::2]
    seconds = order[1::2]
    partners = jnp.zeros((PARTS_SIZE,), jnp.int32)
    partners = partners.at[firsts].set(seconds).at[seconds].set(firsts)
    return partners


def place_ends(entries, own_key, smallest, high):
    longest = entries.shape.index(max(entries.shape))
    spots = []
    for shift in (0, 1):
        where = [jax.random.randint(jax.random.fold_in(own_key, axis), (), 0, length) for axis, length in enumerate(entries.shape)]
        where[longest] = (where[longest] + shift) % entries.shape[longest]
        spots.append(tuple(where))
    return entries.at[spots[0]].set(smallest).at[spots[1]].set(high)


def shard_levels(stream_key, dims, pieces, smallest, top_value):
    level = 1.0
    for position, blocks in pieces:
        steps = jax.random.uniform(jax.random.fold_in(jax.random.fold_in(stream_key, 6), position), (blocks,), jnp.float32, smallest / len(pieces), top_value / len(pieces))
        level = level * jnp.repeat(jnp.exp(steps), dims[position] // blocks).reshape((-1,) + (1,) * (len(dims) - 1 - position))
    return level


def rank_bounds(number_of, skew):
    weights = [(1 << 20) // math.isqrt(standing ** skew) + 1 for standing in range(1, number_of + 1)]
    spread = 1 + sum(weights) // (1 << 30)
    return np.cumsum(np.array([max(1, weight // spread) for weight in weights]))


def ranked(own_key, shape, count, slope):
    grid = rank_bounds(count, slope)
    ticket = jax.random.randint(jax.random.fold_in(own_key, 1), shape, 0, int(grid[count - 1]))
    grade = jnp.searchsorted(jnp.asarray(grid, jnp.int32), ticket, side="right")
    return jax.random.permutation(jax.random.fold_in(own_key, 2), count)[grade].astype(jnp.int32)


def gaussian(key, shape, width, bound, pieces=(), held_as=jnp.bfloat16):
    drawn = jax.random.normal(key, shape, jnp.float32) * width
    if len(pieces) > 0:
        drawn = shard_levels(key, shape, pieces, -0.22, 0.18) * drawn
    return jnp.clip(drawn, min=-bound, max=bound).astype(held_as)


def setup_inputs(seed: int = 0) -> dict:
    splits = jax.random.split(jax.random.key(seed), 13)
    return {
        "source": gaussian(splits[0], (TOTAL_BLOCKS, BW), 1.0, 6.0, ((0, 256),)),
        "lam_init": gaussian(splits[1], (TOTAL_BLOCKS, BW), 1.0, 6.0, ((0, 256),)),
        "offd": gaussian(splits[2], (TOTAL_BLOCKS, BW, K * BW), (BW * K) ** -0.5, 0.1875, ((0, 256),)),
        "dinv": gaussian(splits[3], (BW, TOTAL_BLOCKS * BW), BW ** -0.5, 0.4375, ((1, 256),)),
        "colidx": place_ends(jax.random.randint(splits[4], (TOTAL_BLOCKS, K), 0, PB + FB), jax.random.fold_in(splits[4], 1), 0, (PB + FB) - 1).astype(jnp.int32),
        "face_list": place_ends(jax.random.randint(splits[5], (PARTS_SIZE, FB), 0, PB), jax.random.fold_in(splits[5], 1), 0, PB - 1).astype(jnp.int32),
        "partner": draw_partner(jax.random.fold_in(splits[12], 71), 0),
        "perf_block": place_ends(jax.random.randint(splits[7], (TOTAL_PERF,), 0, BD), jax.random.fold_in(splits[7], 1), 0, BD - 1).astype(jnp.int32),
        "perf_well": place_ends(ranked(splits[8], (TOTAL_PERF,), WP, 2), jax.random.fold_in(splits[8], 3), 0, WP - 1).astype(jnp.int32),
        "perf_sens": gaussian(splits[9], (TOTAL_PERF, BW), (BW * 4) ** -0.5, 0.21875, ((0, 256),)),
        "obj_weight": jnp.clip(jnp.exp(jax.random.uniform(splits[10], (CK,), jnp.float32, math.log(0.5), math.log(2.0))), 0.5, 2.0),
        "step_index": jax.random.randint(splits[11], (1,), 0, CK).astype(jnp.int32),
    }


def coupled_sweep(state, forcing, offd, dinv, colidx, face_list, partner):
    part_count = face_list.shape[0]
    blocks = state.reshape(part_count, -1, BW)
    face_rows = jnp.take_along_axis(blocks, face_list[:, :, None], axis=1)
    halos = face_rows[partner]
    extended = jnp.concatenate([blocks, halos], axis=1)
    inverses = dinv.reshape(BW, -1, BW).transpose(1, 0, 2)

    def one_part(items):
        wide_state, force_part, coupling, inverse, columns = items
        picked = wide_state[columns].reshape(columns.shape[0], K * BW).astype(jnp.float32)
        coupled = jnp.einsum("bim,bm->bi", coupling.astype(jnp.float32), picked)
        residual_rhs = (force_part - coupled).astype(jnp.bfloat16)
        return jnp.einsum("bij,bj->bi", inverse.astype(jnp.float32), residual_rhs.astype(jnp.float32))

    result = lax.map(one_part, (extended, forcing.reshape(part_count, -1, BW), offd.reshape(part_count, -1, BW, K * BW), inverses.reshape(part_count, -1, BW, BW), colidx.reshape(part_count, -1, K)))
    return result.reshape(-1, BW)


def reference(source, lam_init, offd, dinv, colidx, face_list, partner, perf_block, perf_well, perf_sens, obj_weight, step_index):
    weight = obj_weight[step_index[0]]
    forcing = weight * source.astype(jnp.float32)
    first_pass = coupled_sweep(lam_init, forcing, offd, dinv, colidx, face_list, partner).astype(jnp.bfloat16)
    adjoint = coupled_sweep(first_pass, forcing, offd, dinv, colidx, face_list, partner)
    owner_dev = jnp.arange(perf_block.shape[0], dtype=jnp.int32) // PD
    block_rows = owner_dev * BD + perf_block
    well_ids = (owner_dev // N_BLK) * WP + perf_well
    contrib = jnp.sum(perf_sens.astype(jnp.float32) * adjoint[block_rows], axis=1)
    control_grad = -jax.ops.segment_sum(contrib, well_ids, num_segments=PARTS_SIZE * WP)
    return (adjoint, control_grad)
```

```python
import jax
import jax.numpy as jnp
from jax import lax
from jax.experimental import pallas as pl
from jax.experimental.pallas import tpu as pltpu
from jax.sharding import PartitionSpec as P

N_DOM = 32
N_BLK = 8
BD = 16
BW = 192
K = 6
PB = 128
FB = 64
BF = jnp.bfloat16
F32 = jnp.float32


def nt_dot(a, b):
    return lax.dot_general(a, b, (((1,), (1,)), ((), ())), preferred_element_type=F32)


def sweep(z_ref, face_ref, colidx_ref, source_ref, weight_ref, offd_ref, dinv_ref):
    main = z_ref[:, 0:32, :].reshape(N_BLK * 32, 128)
    tails = z_ref[:, 32:48, :].reshape(N_BLK * 16, 128)
    face = face_ref[0, 48:64, :].astype(F32)[0:1, 0:FB]
    columns = colidx_ref[...]
    lane_face = lax.broadcasted_iota(jnp.int32, (BD, FB), 1)
    lane_main = lax.broadcasted_iota(jnp.int32, (BD, N_BLK * 32), 1)
    lane_tail = lax.broadcasted_iota(jnp.int32, (BD, N_BLK * 16), 1)
    hot_main, hot_tail, upper = [], [], []
    for k in range(K):
        c = columns[:, k : k + 1]
        seen = jnp.where(lane_face == c - PB, face, 0.0)
        halo = jnp.sum(seen, axis=1, keepdims=True).astype(jnp.int32)
        other = (c >= PB).astype(jnp.int32)
        block = jnp.where(c >= PB, halo, c)
        dev, row = block // BD, block % BD
        hot_main.append(jnp.where(lane_main == dev * 32 + other * 16 + row, 1.0, 0.0))
        hot_tail.append(jnp.where(lane_tail == dev * 16 + other * 8 + row % 8, 1.0, 0.0))
        upper.append(jnp.broadcast_to(row, (BD, 64)) >= 8)
    got_main = jnp.dot(jnp.concatenate(hot_main, axis=0).astype(BF), main, preferred_element_type=F32)
    got_tail = jnp.dot(jnp.concatenate(hot_tail, axis=0).astype(BF), tails, preferred_element_type=F32)
    pieces = []
    for k in range(K):
        rows = slice(k * BD, (k + 1) * BD)
        tail = got_tail[rows]
        pieces.append(got_main[rows])
        pieces.append(jnp.where(upper[k], tail[:, 64:128], tail[:, 0:64]))
    picked = jnp.concatenate(pieces, axis=1).astype(BF)

    forcing = source_ref[...].astype(F32) * weight_ref[0]
    forcing = jnp.concatenate([forcing, forcing], axis=1)
    row_id = lax.broadcasted_iota(jnp.int32, (BD, 2 * BW), 0)
    half = (lax.broadcasted_iota(jnp.int32, (BD, 2 * BW), 1) >= BW).astype(jnp.int32)
    total = jnp.zeros((BD, BW), F32)
    for pair in range(BD // 2):
        coupling = offd_ref[2 * pair : 2 * pair + 2].reshape(2 * BW, K * BW)
        coupled = nt_dot(picked, coupling)
        rhs = jnp.where(row_id == half + 2 * pair, forcing - coupled, 0.0).astype(BF)
        total = total + nt_dot(rhs, dinv_ref[:, 2 * pair * BW : 2 * (pair + 1) * BW])
    return total


def first_kernel(weight_ref, z_ref, colidx_ref, source_ref, offd_ref, dinv_ref, out_ref):
    total = sweep(z_ref, z_ref, colidx_ref, source_ref, weight_ref, offd_ref, dinv_ref)
    packed = jnp.concatenate(
        [total[:, 0:128], jnp.concatenate([total[0:8, 128:192], total[8:16, 128:192]], axis=1)], axis=0
    )
    out_ref[...] = packed.astype(BF)


def last_kernel(
    weight_ref, z_ref, face_ref, colidx_ref, source_ref, offd_ref, dinv_ref, sens_ref, block_ref, well_ref, adj_ref, sum_ref
):
    total = sweep(z_ref, face_ref, colidx_ref, source_ref, weight_ref, offd_ref, dinv_ref)
    adj_ref[...] = total
    sens = sens_ref[...]
    high = total.astype(BF)
    rest = total - high.astype(F32)
    low = rest.astype(BF)
    lowest = (rest - low.astype(F32)).astype(BF)
    dots = nt_dot(high, sens) + nt_dot(low, sens) + nt_dot(lowest, sens)
    perf = dots.shape[1]
    row_id = lax.broadcasted_iota(jnp.int32, (BD, perf), 0)
    contrib = jnp.sum(jnp.where(row_id == block_ref[...], dots, 0.0), axis=0, keepdims=True)
    well = well_ref[...]
    target = lax.broadcasted_iota(jnp.int32, (N_BLK, perf), 0)
    spread = jnp.where(target == well // 8, -contrib, 0.0)
    lane = lax.broadcasted_iota(jnp.int32, (128, perf), 0)
    hot = jnp.where(lane == well % 8, 1.0, 0.0).astype(BF)
    high = spread.astype(BF)
    rest = spread - high.astype(F32)
    low = rest.astype(BF)
    lowest = (rest - low.astype(F32)).astype(BF)
    sum_ref[...] = nt_dot(high, hot) + nt_dot(low, hot) + nt_dot(lowest, hot)


def pack(rows):
    tails = jnp.concatenate([rows[0:8, 128:192], rows[8:16, 128:192]], axis=1)
    return jnp.concatenate([rows[:, 0:128], tails], axis=0)


def from_partner(message, partner_id):
    sent = jnp.broadcast_to(message[None], (N_DOM,) + message.shape)
    incoming = lax.all_to_all(sent, "dom", split_axis=0, concat_axis=0, tiled=True)
    return lax.dynamic_index_in_dim(incoming, partner_id, 0, keepdims=False)


def to_all(message):
    sent = jnp.broadcast_to(message[None], (N_BLK,) + message.shape)
    return lax.all_to_all(sent, "blk", split_axis=0, concat_axis=0, tiled=True)


def body(
    source,
    lam_init,
    offd,
    dinv,
    colidx,
    face_list,
    partner,
    perf_block,
    perf_well,
    perf_sens,
    obj_weight,
    step_index,
):
    partner_id = partner[0]
    weight = lax.dynamic_slice(obj_weight, (step_index[0],), (1,))
    own = pack(lam_init)
    faces = jnp.pad(face_list.astype(BF), ((0, 7), (0, 64)))
    got = from_partner(jnp.concatenate([own, faces], axis=0), partner_id)
    z1 = to_all(
        jnp.concatenate(
            [own[0:16], got[0:16], own[16:24], got[16:24], got[24:32], jnp.zeros((8, 128), BF)], axis=0
        )
    )
    vmem = pl.BlockSpec(memory_space=pltpu.VMEM)
    smem = pl.BlockSpec(memory_space=pltpu.SMEM)
    limit = pltpu.CompilerParams(vmem_limit_bytes=40 * 1024 * 1024)
    own = pl.pallas_call(
        first_kernel,
        out_shape=jax.ShapeDtypeStruct((24, 128), BF),
        in_specs=[smem] + [vmem] * 5,
        out_specs=vmem,
        compiler_params=limit,
    )(weight, z1, colidx, source, offd, dinv)
    got = from_partner(own, partner_id)
    z2 = to_all(jnp.concatenate([own[0:16], got[0:16], own[16:24], got[16:24]], axis=0))
    perf = perf_block.shape[0]
    adjoint, sums = pl.pallas_call(
        last_kernel,
        out_shape=(jax.ShapeDtypeStruct((BD, BW), F32), jax.ShapeDtypeStruct((N_BLK, 128), F32)),
        in_specs=[smem] + [vmem] * 9,
        out_specs=(vmem, vmem),
        compiler_params=limit,
    )(
        weight,
        z2,
        z1,
        colidx,
        source,
        offd,
        dinv,
        perf_sens,
        perf_block.reshape(1, perf),
        perf_well.reshape(1, perf),
    )
    terms = lax.all_to_all(sums, "blk", split_axis=0, concat_axis=0, tiled=True)
    control_grad = jnp.sum(terms, axis=0)[0:8]
    return (adjoint, control_grad)


def solution(mesh):
    placed = (
        P(("dom", "blk"), None),
        P(("dom", "blk"), None),
        P(("dom", "blk"), None, None),
        P(None, ("dom", "blk")),
        P(("dom", "blk"), None),
        P("dom", None),
        P("dom"),
        P(("dom", "blk")),
        P(("dom", "blk")),
        P(("dom", "blk"), None),
        P(),
        P(),
    )
    return jax.shard_map(
        body,
        mesh=mesh,
        in_specs=placed,
        out_specs=(P(("dom", "blk"), None), P(("dom", "blk"))),
        check_vma=False,
    )
```

```python
import jax
import jax.numpy as jnp
from jax import lax
from jax.experimental import pallas as pl
from jax.experimental.pallas import tpu as pltpu
from jax.sharding import PartitionSpec as P

N_DOM = 32
N_BLK = 8
BD = 16
BW = 192
K = 6
PB = 128
FB = 64
GROUP = 4
BF = jnp.bfloat16
F32 = jnp.float32


def nt_dot(a, b):
    return lax.dot_general(a, b, (((1,), (1,)), ((), ())), preferred_element_type=F32)


def packed(rows):
    tails = jnp.concatenate([rows[0:8, 128:192], rows[8:16, 128:192]], axis=1)
    return jnp.concatenate([rows[:, 0:128], tails], axis=0)


def three_parts(x):
    high = x.astype(BF)
    rest = x - high.astype(F32)
    mid = rest.astype(BF)
    return high, mid, (rest - mid.astype(F32)).astype(BF)


def entry_kernel(lam_hbm, face_hbm, message_ref, own_ref, lam_ref, face_ref, sems):
    copies = [pltpu.make_async_copy(lam_hbm, lam_ref, sems.at[0]), pltpu.make_async_copy(face_hbm, face_ref, sems.at[1])]
    for copy in copies:
        copy.start()
    for copy in copies:
        copy.wait()
    own = packed(lam_ref[...].astype(F32))
    face = jnp.concatenate([face_ref[...].astype(F32), jnp.zeros((1, 64), F32)], axis=1)
    message = jnp.concatenate([own, jnp.broadcast_to(face, (8, 128))], axis=0).astype(BF)
    own_ref[...] = message
    for slot in range(N_DOM):
        message_ref[slot] = message


def select_kernel(scalars_ref, incoming_ref, own_ref, *refs):
    out_ref = refs[-1]
    got = incoming_ref[jnp.max(scalars_ref[:, 0:1])].astype(F32)
    own = own_ref[...].astype(F32)
    rows = [own[0:16], got[0:16], own[16:24], got[16:24]]
    if out_ref.shape[1] > 48:
        rows.append(got[24:32])
    message = jnp.concatenate(rows, axis=0).astype(BF)
    for slot in range(N_BLK):
        out_ref[slot] = message


def gather_tables(face, columns, main_ref, tail_ref, upper_ref):
    lane_face = lax.broadcasted_iota(jnp.int32, (BD, FB), 1)
    lane_main = lax.broadcasted_iota(jnp.int32, (BD, N_BLK * 32), 1)
    lane_tail = lax.broadcasted_iota(jnp.int32, (BD, N_BLK * 16), 1)
    for k in range(K):
        rows = slice(k * BD, (k + 1) * BD)
        c = columns[:, k : k + 1]
        seen = jnp.where(lane_face == c - PB, face, 0.0)
        halo = jnp.sum(seen, axis=1, keepdims=True).astype(jnp.int32)
        other = (c >= PB).astype(jnp.int32)
        block = jnp.where(c >= PB, halo, c)
        dev, row = block // BD, block % BD
        main_ref[rows, :] = jnp.where(lane_main == dev * 32 + other * 16 + row, 1.0, 0.0).astype(BF)
        tail_ref[rows, :] = jnp.where(lane_tail == dev * 16 + other * 8 + row % 8, 1.0, 0.0).astype(BF)
        upper_ref[rows, :] = jnp.broadcast_to(row // 8, (BD, 64))


def sweep(z_ref, main_ref, tail_ref, upper_ref, forcing, offd, dinv):
    main = z_ref[:, 0:32, :].reshape(N_BLK * 32, 128)
    tails = z_ref[:, 32:48, :].reshape(N_BLK * 16, 128)
    got_main = jnp.dot(main_ref[...], main, preferred_element_type=F32)
    got_tail = jnp.dot(tail_ref[...], tails, preferred_element_type=F32)
    got_tail = jnp.where(upper_ref[...] > 0, got_tail[:, 64:128], got_tail[:, 0:64])
    pieces = []
    for k in range(K):
        rows = slice(k * BD, (k + 1) * BD)
        pieces.append(got_main[rows])
        pieces.append(got_tail[rows])
    picked = jnp.concatenate(pieces, axis=1).astype(BF)

    width = GROUP * BW
    forcing = jnp.concatenate([forcing] * GROUP, axis=1)
    row_id = lax.broadcasted_iota(jnp.int32, (BD, width), 0)
    part = lax.broadcasted_iota(jnp.int32, (BD, width), 1) // BW
    total = jnp.zeros((BD, BW), F32)
    for first in range(0, BD, GROUP):
        coupled = nt_dot(picked, offd[first : first + GROUP].reshape(width, K * BW))
        rhs = jnp.where(row_id == part + first, forcing - coupled, 0.0).astype(BF)
        total = total + nt_dot(rhs, dinv[:, first * BW : (first + GROUP) * BW])
    return total


def first_kernel(
    scalars_ref,
    z_ref,
    columns_ref,
    source_ref,
    weights_ref,
    offd,
    dinv,
    out_ref,
    own_ref,
    forcing_ref,
    main_ref,
    tail_ref,
    upper_ref,
    square,
):
    square[0:K, 0:BD] = columns_ref[...]
    columns = square[...].T[0:BD, :]
    face = z_ref[0].astype(F32)[48:49, 0:FB]
    gather_tables(face, columns, main_ref, tail_ref, upper_ref)
    number = lax.broadcasted_iota(jnp.int32, (8, 128), 0) * 128 + lax.broadcasted_iota(jnp.int32, (8, 128), 1)
    weight = jnp.sum(jnp.where(number == scalars_ref[:, 1:2], weights_ref[...], 0.0), keepdims=True)
    forcing = source_ref[...].astype(F32) * weight
    forcing_ref[...] = forcing
    total = sweep(z_ref, main_ref, tail_ref, upper_ref, forcing, offd, dinv)
    message = packed(total).astype(BF)
    own_ref[...] = message
    for slot in range(N_DOM):
        out_ref[slot] = message


def last_kernel(
    z_ref, main_ref, tail_ref, upper_ref, forcing_ref, sens_ref, block_ref, well_ref, offd, dinv, adj_ref, sum_ref
):
    total = sweep(z_ref, main_ref, tail_ref, upper_ref, forcing_ref[...], offd, dinv)
    adj_ref[...] = total
    sens = sens_ref[...]
    dots = sum(jnp.dot(part, sens, preferred_element_type=F32) for part in three_parts(total))
    perf = dots.shape[1]
    row_id = lax.broadcasted_iota(jnp.int32, (BD, perf), 0)
    contrib = jnp.sum(jnp.where(row_id == block_ref[...], dots, 0.0), axis=0, keepdims=True)
    well = well_ref[...]
    target = lax.broadcasted_iota(jnp.int32, (N_BLK, perf), 0)
    spread = jnp.where(target == well // 8, -contrib, 0.0)
    lane = lax.broadcasted_iota(jnp.int32, (128, perf), 0)
    hot = jnp.where(lane == well % 8, 1.0, 0.0).astype(BF)
    sum_ref[...] = sum(nt_dot(part, hot) for part in three_parts(spread))


def shift(message, axis):
    return lax.all_to_all(message, axis, split_axis=0, concat_axis=0, tiled=True)


def in_hbm(x):
    return pltpu.with_memory_space_constraint(x, pltpu.HBM)


def body(
    source,
    lam_init,
    offd,
    dinv,
    colidx,
    face_list,
    partner,
    perf_block,
    perf_well,
    perf_sens,
    obj_weight,
    step_index,
):
    vmem = pl.BlockSpec(memory_space=pltpu.VMEM)
    hbm = pl.BlockSpec(memory_space=pltpu.HBM)

    def shape(dims, dtype):
        return jax.ShapeDtypeStruct(dims, dtype)

    limit = pltpu.CompilerParams(vmem_limit_bytes=4 * 1024 * 1024)
    small = pltpu.CompilerParams(vmem_limit_bytes=4 * 1024 * 1024)
    message, own = pl.pallas_call(
        entry_kernel,
        out_shape=(shape((N_DOM, 32, 128), BF), shape((32, 128), BF)),
        in_specs=[hbm] * 2,
        out_specs=[vmem] * 2,
        scratch_shapes=[pltpu.VMEM((BD, BW), BF), pltpu.VMEM((1, FB), jnp.int32), pltpu.SemaphoreType.DMA((2,))],
        compiler_params=small,
    )(in_hbm(lam_init), in_hbm(face_list))
    scalars = jnp.concatenate([partner, step_index]).reshape(1, 2)

    def spread(incoming, own, rows, *unread):
        return pl.pallas_call(
            select_kernel,
            out_shape=shape((N_BLK, rows, 128), BF),
            in_specs=[vmem] * 3 + [hbm] * len(unread),
            out_specs=vmem,
            compiler_params=small,
        )(scalars, incoming, own, *unread)

    z1 = shift(spread(shift(message, "dom"), own, 56, in_hbm(offd), in_hbm(dinv)), "blk")
    message, own, forcing, *tables = pl.pallas_call(
        first_kernel,
        out_shape=(
            shape((N_DOM, 24, 128), BF),
            shape((24, 128), BF),
            shape((BD, BW), F32),
            shape((K * BD, N_BLK * 32), BF),
            shape((K * BD, N_BLK * 16), BF),
            shape((K * BD, 64), jnp.int32),
        ),
        in_specs=[vmem] * 7,
        out_specs=[vmem] * 6,
        scratch_shapes=[pltpu.VMEM((128, 128), jnp.int32)],
        compiler_params=limit,
    )(scalars, z1, colidx.T, source, obj_weight.reshape(8, 128), offd, dinv)
    z2 = shift(spread(shift(message, "dom"), own, 48), "blk")
    perf = perf_block.shape[0]
    adjoint, sums = pl.pallas_call(
        last_kernel,
        out_shape=(shape((BD, BW), F32), shape((N_BLK, 128), F32)),
        in_specs=[vmem] * 10,
        out_specs=(vmem, vmem),
        compiler_params=limit,
    )(
        z2,
        *tables,
        forcing,
        perf_sens.T,
        perf_block.reshape(1, perf),
        perf_well.reshape(1, perf),
        offd,
        dinv,
    )
    control_grad = jnp.sum(shift(sums, "blk"), axis=0)[0:8]
    return (adjoint, control_grad)


def solution(mesh):
    placed = (
        P(("dom", "blk"), None),
        P(("dom", "blk"), None),
        P(("dom", "blk"), None, None),
        P(None, ("dom", "blk")),
        P(("dom", "blk"), None),
        P("dom", None),
        P("dom"),
        P(("dom", "blk")),
        P(("dom", "blk")),
        P(("dom", "blk"), None),
        P(),
        P(),
    )
    return jax.shard_map(
        body,
        mesh=mesh,
        in_specs=placed,
        out_specs=(P(("dom", "blk"), None), P(("dom", "blk"))),
        check_vma=False,
    )
```

```python
import jax
import jax.numpy as jnp
from jax import lax
from jax.experimental import pallas as pl
from jax.experimental.pallas import tpu as pltpu
from jax.sharding import PartitionSpec as P

N_DOM = 32
N_BLK = 8
BD = 16
BW = 192
K = 6
PB = 128
FB = 64
GROUP = 4
BF = jnp.bfloat16
F32 = jnp.float32


def nt_dot(a, b):
    return lax.dot_general(a, b, (((1,), (1,)), ((), ())), preferred_element_type=F32)


def packed(rows):
    tails = jnp.concatenate([rows[0:8, 128:192], rows[8:16, 128:192]], axis=1)
    return jnp.concatenate([rows[:, 0:128], tails], axis=0)


def three_parts(x):
    high = x.astype(BF)
    rest = x - high.astype(F32)
    mid = rest.astype(BF)
    return high, mid, (rest - mid.astype(F32)).astype(BF)


def entry_kernel(lam_hbm, face_hbm, message_ref, own_ref, lam_ref, face_ref, sems):
    copies = [pltpu.make_async_copy(lam_hbm, lam_ref, sems.at[0]), pltpu.make_async_copy(face_hbm, face_ref, sems.at[1])]
    for copy in copies:
        copy.start()
    for copy in copies:
        copy.wait()
    own = packed(lam_ref[...].astype(F32))
    face = jnp.concatenate([face_ref[...].astype(F32), jnp.zeros((1, 64), F32)], axis=1)
    message = jnp.concatenate([own, jnp.broadcast_to(face, (8, 128))], axis=0).astype(BF)
    own_ref[...] = message
    for slot in range(N_DOM):
        message_ref[slot] = message


def select_kernel(scalars_ref, incoming_ref, own_ref, *refs):
    out_ref = refs[-1]
    got = incoming_ref[jnp.max(scalars_ref[:, 0:1])].astype(F32)
    own = own_ref[...].astype(F32)
    rows = [own[0:16], got[0:16], own[16:24], got[16:24]]
    if out_ref.shape[1] > 48:
        rows.append(got[24:32])
    message = jnp.concatenate(rows, axis=0).astype(BF)
    for slot in range(N_BLK):
        out_ref[slot] = message


def gather_tables(face, columns, main_ref, tail_ref, upper_ref):
    lane_face = lax.broadcasted_iota(jnp.int32, (BD, FB), 1)
    lane_main = lax.broadcasted_iota(jnp.int32, (BD, N_BLK * 32), 1)
    lane_tail = lax.broadcasted_iota(jnp.int32, (BD, N_BLK * 16), 1)
    for k in range(K):
        rows = slice(k * BD, (k + 1) * BD)
        c = columns[:, k : k + 1]
        seen = jnp.where(lane_face == c - PB, face, 0.0)
        halo = jnp.sum(seen, axis=1, keepdims=True).astype(jnp.int32)
        other = (c >= PB).astype(jnp.int32)
        block = jnp.where(c >= PB, halo, c)
        dev, row = block // BD, block % BD
        main_ref[rows, :] = jnp.where(lane_main == dev * 32 + other * 16 + row, 1.0, 0.0).astype(BF)
        tail_ref[rows, :] = jnp.where(lane_tail == dev * 16 + other * 8 + row % 8, 1.0, 0.0).astype(BF)
        upper_ref[rows, :] = jnp.broadcast_to(row // 8, (BD, 64))


def sweep(z_ref, main_ref, tail_ref, upper_ref, forcing, offd, dinv):
    main = z_ref[:, 0:32, :].reshape(N_BLK * 32, 128)
    tails = z_ref[:, 32:48, :].reshape(N_BLK * 16, 128)
    got_main = jnp.dot(main_ref[...], main, preferred_element_type=F32)
    got_tail = jnp.dot(tail_ref[...], tails, preferred_element_type=F32)
    got_tail = jnp.where(upper_ref[...] > 0, got_tail[:, 64:128], got_tail[:, 0:64])
    pieces = []
    for k in range(K):
        rows = slice(k * BD, (k + 1) * BD)
        pieces.append(got_main[rows])
        pieces.append(got_tail[rows])
    picked = jnp.concatenate(pieces, axis=1).astype(BF)

    width = GROUP * BW
    forcing = jnp.concatenate([forcing] * GROUP, axis=1)
    row_id = lax.broadcasted_iota(jnp.int32, (BD, width), 0)
    part = lax.broadcasted_iota(jnp.int32, (BD, width), 1) // BW
    total = jnp.zeros((BD, BW), F32)
    for first in range(0, BD, GROUP):
        coupled = nt_dot(picked, offd[first : first + GROUP].reshape(width, K * BW))
        rhs = jnp.where(row_id == part + first, forcing - coupled, 0.0).astype(BF)
        total = total + nt_dot(rhs, dinv[:, first * BW : (first + GROUP) * BW])
    return total


def first_kernel(
    scalars_ref,
    z_ref,
    columns_ref,
    source_ref,
    weights_ref,
    offd,
    dinv,
    out_ref,
    own_ref,
    forcing_ref,
    main_ref,
    tail_ref,
    upper_ref,
    square,
):
    square[0:K, 0:BD] = columns_ref[...]
    columns = square[...].T[0:BD, :]
    face = z_ref[0].astype(F32)[48:49, 0:FB]
    gather_tables(face, columns, main_ref, tail_ref, upper_ref)
    number = lax.broadcasted_iota(jnp.int32, (8, 128), 0) * 128 + lax.broadcasted_iota(jnp.int32, (8, 128), 1)
    weight = jnp.sum(jnp.where(number == scalars_ref[:, 1:2], weights_ref[...], 0.0), keepdims=True)
    forcing = source_ref[...].astype(F32) * weight
    forcing_ref[...] = forcing
    total = sweep(z_ref, main_ref, tail_ref, upper_ref, forcing, offd, dinv)
    message = packed(total).astype(BF)
    own_ref[...] = message
    for slot in range(N_DOM):
        out_ref[slot] = message


def last_kernel(
    z_ref, main_ref, tail_ref, upper_ref, forcing_ref, sens_ref, block_ref, well_ref, offd, dinv, adj_ref, sum_ref
):
    total = sweep(z_ref, main_ref, tail_ref, upper_ref, forcing_ref[...], offd, dinv)
    adj_ref[...] = total
    sens = sens_ref[...]
    dots = sum(jnp.dot(part, sens, preferred_element_type=F32) for part in three_parts(total))
    perf = dots.shape[1]
    row_id = lax.broadcasted_iota(jnp.int32, (BD, perf), 0)
    contrib = jnp.sum(jnp.where(row_id == block_ref[...], dots, 0.0), axis=0, keepdims=True)
    well = well_ref[...]
    target = lax.broadcasted_iota(jnp.int32, (N_BLK, perf), 0)
    spread = jnp.where(target == well // 8, -contrib, 0.0)
    lane = lax.broadcasted_iota(jnp.int32, (128, perf), 0)
    hot = jnp.where(lane == well % 8, 1.0, 0.0).astype(BF)
    sum_ref[...] = sum(nt_dot(part, hot) for part in three_parts(spread))


def shift(message, axis):
    return lax.all_to_all(message, axis, split_axis=0, concat_axis=0, tiled=True)


def result_kernel(terms_ref, total_ref, adj_ref, grad_ref):
    adj_ref[...] = total_ref[...]
    terms = terms_ref[:, 0, :]
    grad_ref[...] = jnp.sum(terms, axis=0, keepdims=True)[:, 0:8]


def in_hbm(x):
    return pltpu.with_memory_space_constraint(x, pltpu.HBM)


def body(
    source,
    lam_init,
    offd,
    dinv,
    colidx,
    face_list,
    partner,
    perf_block,
    perf_well,
    perf_sens,
    obj_weight,
    step_index,
):
    vmem = pl.BlockSpec(memory_space=pltpu.VMEM)
    hbm = pl.BlockSpec(memory_space=pltpu.HBM)

    def shape(dims, dtype):
        return jax.ShapeDtypeStruct(dims, dtype)

    limit = pltpu.CompilerParams(vmem_limit_bytes=4 * 1024 * 1024)
    small = pltpu.CompilerParams(vmem_limit_bytes=4 * 1024 * 1024)
    message, own = pl.pallas_call(
        entry_kernel,
        out_shape=(shape((N_DOM, 32, 128), BF), shape((32, 128), BF)),
        in_specs=[hbm] * 2,
        out_specs=[vmem] * 2,
        scratch_shapes=[pltpu.VMEM((BD, BW), BF), pltpu.VMEM((1, FB), jnp.int32), pltpu.SemaphoreType.DMA((2,))],
        compiler_params=small,
    )(in_hbm(lam_init), in_hbm(face_list))
    scalars = jnp.concatenate([partner, step_index]).reshape(1, 2)

    def spread(incoming, own, rows, *unread):
        return pl.pallas_call(
            select_kernel,
            out_shape=shape((N_BLK, rows, 128), BF),
            in_specs=[vmem] * 3 + [hbm] * len(unread),
            out_specs=vmem,
            compiler_params=small,
        )(scalars, incoming, own, *unread)

    z1 = shift(spread(shift(message, "dom"), own, 56, in_hbm(offd), in_hbm(dinv)), "blk")
    message, own, forcing, *tables = pl.pallas_call(
        first_kernel,
        out_shape=(
            shape((N_DOM, 24, 128), BF),
            shape((24, 128), BF),
            shape((BD, BW), F32),
            shape((K * BD, N_BLK * 32), BF),
            shape((K * BD, N_BLK * 16), BF),
            shape((K * BD, 64), jnp.int32),
        ),
        in_specs=[vmem] * 7,
        out_specs=[vmem] * 6,
        scratch_shapes=[pltpu.VMEM((128, 128), jnp.int32)],
        compiler_params=limit,
    )(scalars, z1, colidx.T, source, obj_weight.reshape(8, 128), offd, dinv)
    z2 = shift(spread(shift(message, "dom"), own, 48), "blk")
    perf = perf_block.shape[0]
    adjoint, sums = pl.pallas_call(
        last_kernel,
        out_shape=(shape((BD, BW), F32), shape((N_BLK, 128), F32)),
        in_specs=[vmem] * 10,
        out_specs=(vmem, vmem),
        compiler_params=limit,
    )(
        z2,
        *tables,
        forcing,
        perf_sens.T,
        perf_block.reshape(1, perf),
        perf_well.reshape(1, perf),
        offd,
        dinv,
    )
    terms = shift(sums.reshape(N_BLK, 1, 128), "blk")
    adjoint, control_grad = pl.pallas_call(
        result_kernel,
        out_shape=(shape((BD, BW), F32), shape((1, 8), F32)),
        in_specs=[vmem] * 2,
        out_specs=(vmem, vmem),
        compiler_params=small,
    )(terms, adjoint)
    return (adjoint, control_grad.reshape(8))


def solution(mesh):
    placed = (
        P(("dom", "blk"), None),
        P(("dom", "blk"), None),
        P(("dom", "blk"), None, None),
        P(None, ("dom", "blk")),
        P(("dom", "blk"), None),
        P("dom", None),
        P("dom"),
        P(("dom", "blk")),
        P(("dom", "blk")),
        P(("dom", "blk"), None),
        P(),
        P(),
    )
    return jax.shard_map(
        body,
        mesh=mesh,
        in_specs=placed,
        out_specs=(P(("dom", "blk"), None), P(("dom", "blk"))),
        check_vma=False,
    )
```

```python
import jax
import jax.numpy as jnp
from jax import lax
from jax.experimental import pallas as pl
from jax.experimental.pallas import tpu as pltpu
from jax.sharding import PartitionSpec as P

N_DOM = 32
N_BLK = 8
BD = 16
BW = 192
K = 6
PB = 128
FB = 64
GROUP = 4
BF = jnp.bfloat16
F32 = jnp.float32


def nt_dot(a, b):
    return lax.dot_general(a, b, (((1,), (1,)), ((), ())), preferred_element_type=F32)


def packed(rows):
    tails = jnp.concatenate([rows[0:8, 128:192], rows[8:16, 128:192]], axis=1)
    return jnp.concatenate([rows[:, 0:128], tails], axis=0)


def three_parts(x):
    high = x.astype(BF)
    rest = x - high.astype(F32)
    mid = rest.astype(BF)
    return high, mid, (rest - mid.astype(F32)).astype(BF)


def entry_kernel(lam_hbm, face_hbm, message_ref, own_ref, lam_ref, face_ref, sems):
    copies = [pltpu.make_async_copy(lam_hbm, lam_ref, sems.at[0]), pltpu.make_async_copy(face_hbm, face_ref, sems.at[1])]
    for copy in copies:
        copy.start()
    for copy in copies:
        copy.wait()
    own = packed(lam_ref[...].astype(F32))
    face = jnp.concatenate([face_ref[...].astype(F32), jnp.zeros((1, 64), F32)], axis=1)
    message = jnp.concatenate([own, jnp.broadcast_to(face, (8, 128))], axis=0).astype(BF)
    own_ref[...] = message
    for slot in range(N_DOM):
        message_ref[slot] = message


def select_kernel(scalars_ref, incoming_ref, own_ref, *refs):
    out_ref = refs[-1]
    got = incoming_ref[jnp.max(scalars_ref[:, 0:1])].astype(F32)
    own = own_ref[...].astype(F32)
    rows = [own[0:16], got[0:16], own[16:24], got[16:24]]
    if out_ref.shape[1] > 48:
        rows.append(got[24:32])
    message = jnp.concatenate(rows, axis=0).astype(BF)
    for slot in range(N_BLK):
        out_ref[slot] = message


def gather_tables(face, columns, main_ref, tail_ref, upper_ref):
    lane_face = lax.broadcasted_iota(jnp.int32, (BD, FB), 1)
    lane_main = lax.broadcasted_iota(jnp.int32, (BD, N_BLK * 32), 1)
    lane_tail = lax.broadcasted_iota(jnp.int32, (BD, N_BLK * 16), 1)
    for k in range(K):
        rows = slice(k * BD, (k + 1) * BD)
        c = columns[:, k : k + 1]
        seen = jnp.where(lane_face == c - PB, face, 0.0)
        halo = jnp.sum(seen, axis=1, keepdims=True).astype(jnp.int32)
        other = (c >= PB).astype(jnp.int32)
        block = jnp.where(c >= PB, halo, c)
        dev, row = block // BD, block % BD
        main_ref[rows, :] = jnp.where(lane_main == dev * 32 + other * 16 + row, 1.0, 0.0).astype(BF)
        tail_ref[rows, :] = jnp.where(lane_tail == dev * 16 + other * 8 + row % 8, 1.0, 0.0).astype(BF)
        upper_ref[rows, :] = jnp.broadcast_to(row // 8, (BD, 64))


def sweep(z_ref, main_ref, tail_ref, upper_ref, forcing, offd, dinv):
    main = z_ref[:, 0:32, :].reshape(N_BLK * 32, 128)
    tails = z_ref[:, 32:48, :].reshape(N_BLK * 16, 128)
    got_main = jnp.dot(main_ref[...], main, preferred_element_type=F32)
    got_tail = jnp.dot(tail_ref[...], tails, preferred_element_type=F32)
    got_tail = jnp.where(upper_ref[...] > 0, got_tail[:, 64:128], got_tail[:, 0:64])
    width = GROUP * BW
    forcing = jnp.concatenate([forcing] * GROUP, axis=1)
    row_id = lax.broadcasted_iota(jnp.int32, (BD, width), 0)
    part = lax.broadcasted_iota(jnp.int32, (BD, width), 1) // BW
    pieces = []
    for pair in range(K // 2):
        first, second = (slice(k * BD, (k + 1) * BD) for k in (2 * pair, 2 * pair + 1))
        pieces.append(got_main[first])
        pieces.append(jnp.concatenate([got_tail[first], got_main[second][:, 0:64]], axis=1))
        pieces.append(jnp.concatenate([got_main[second][:, 64:128], got_tail[second]], axis=1))
    ones = jnp.ones((BD, 128), BF)
    total = jnp.zeros((BD, BW), F32)
    for first in range(0, BD, GROUP):
        coupled = []
        for block in range(first, first + GROUP):
            factors = [jnp.broadcast_to(piece[block : block + 1, :], (16, 128)) for piece in pieces]
            lanes = []
            for row in range(0, BW, 16):
                partial = None
                for tile, factor in enumerate(factors):
                    term = offd[block, row : row + 16, tile * 128 : (tile + 1) * 128].astype(F32) * factor
                    partial = term if partial is None else partial + term
                lanes.append(partial)
            lanes = jnp.concatenate(lanes, axis=0)
            high = lanes.astype(BF)
            coupled.append(nt_dot(ones, high) + nt_dot(ones, (lanes - high.astype(F32)).astype(BF)))
        coupled = jnp.concatenate(coupled, axis=1)
        rhs = jnp.where(row_id == part + first, forcing - coupled, 0.0).astype(BF)
        total = total + nt_dot(rhs, dinv[:, first * BW : (first + GROUP) * BW])
    return total


def first_kernel(
    scalars_ref,
    z_ref,
    columns_ref,
    source_ref,
    weights_ref,
    offd,
    dinv,
    out_ref,
    own_ref,
    forcing_ref,
    main_ref,
    tail_ref,
    upper_ref,
    square,
):
    square[0:K, 0:BD] = columns_ref[...]
    columns = square[...].T[0:BD, :]
    face = z_ref[0].astype(F32)[48:49, 0:FB]
    gather_tables(face, columns, main_ref, tail_ref, upper_ref)
    number = lax.broadcasted_iota(jnp.int32, (8, 128), 0) * 128 + lax.broadcasted_iota(jnp.int32, (8, 128), 1)
    weight = jnp.sum(jnp.where(number == scalars_ref[:, 1:2], weights_ref[...], 0.0), keepdims=True)
    forcing = source_ref[...].astype(F32) * weight
    forcing_ref[...] = forcing
    total = sweep(z_ref, main_ref, tail_ref, upper_ref, forcing, offd, dinv)
    message = packed(total).astype(BF)
    own_ref[...] = message
    for slot in range(N_DOM):
        out_ref[slot] = message


def last_kernel(
    z_ref, main_ref, tail_ref, upper_ref, forcing_ref, sens_ref, block_ref, well_ref, offd, dinv, adj_ref, sum_ref
):
    total = sweep(z_ref, main_ref, tail_ref, upper_ref, forcing_ref[...], offd, dinv)
    adj_ref[...] = total
    sens = sens_ref[...]
    dots = sum(jnp.dot(part, sens, preferred_element_type=F32) for part in three_parts(total))
    perf = dots.shape[1]
    row_id = lax.broadcasted_iota(jnp.int32, (BD, perf), 0)
    contrib = jnp.sum(jnp.where(row_id == block_ref[...], dots, 0.0), axis=0, keepdims=True)
    well = well_ref[...]
    target = lax.broadcasted_iota(jnp.int32, (N_BLK, perf), 0)
    spread = jnp.where(target == well // 8, -contrib, 0.0)
    lane = lax.broadcasted_iota(jnp.int32, (128, perf), 0)
    hot = jnp.where(lane == well % 8, 1.0, 0.0).astype(BF)
    sum_ref[...] = sum(nt_dot(part, hot) for part in three_parts(spread))


def shift(message, axis):
    return lax.all_to_all(message, axis, split_axis=0, concat_axis=0, tiled=True)


def result_kernel(terms_ref, total_ref, adj_ref, grad_ref):
    adj_ref[...] = total_ref[...]
    terms = terms_ref[:, 0, :]
    grad_ref[...] = jnp.sum(terms, axis=0, keepdims=True)[:, 0:8]


def in_hbm(x):
    return pltpu.with_memory_space_constraint(x, pltpu.HBM)


def body(
    source,
    lam_init,
    offd,
    dinv,
    colidx,
    face_list,
    partner,
    perf_block,
    perf_well,
    perf_sens,
    obj_weight,
    step_index,
):
    vmem = pl.BlockSpec(memory_space=pltpu.VMEM)
    hbm = pl.BlockSpec(memory_space=pltpu.HBM)

    def shape(dims, dtype):
        return jax.ShapeDtypeStruct(dims, dtype)

    limit = pltpu.CompilerParams(vmem_limit_bytes=4 * 1024 * 1024)
    small = pltpu.CompilerParams(vmem_limit_bytes=4 * 1024 * 1024)
    message, own = pl.pallas_call(
        entry_kernel,
        out_shape=(shape((N_DOM, 32, 128), BF), shape((32, 128), BF)),
        in_specs=[hbm] * 2,
        out_specs=[vmem] * 2,
        scratch_shapes=[pltpu.VMEM((BD, BW), BF), pltpu.VMEM((1, FB), jnp.int32), pltpu.SemaphoreType.DMA((2,))],
        compiler_params=small,
    )(in_hbm(lam_init), in_hbm(face_list))
    scalars = jnp.concatenate([partner, step_index]).reshape(1, 2)

    def spread(incoming, own, rows, *unread):
        return pl.pallas_call(
            select_kernel,
            out_shape=shape((N_BLK, rows, 128), BF),
            in_specs=[vmem] * 3 + [hbm] * len(unread),
            out_specs=vmem,
            compiler_params=small,
        )(scalars, incoming, own, *unread)

    z1 = shift(spread(shift(message, "dom"), own, 56, in_hbm(offd), in_hbm(dinv)), "blk")
    message, own, forcing, *tables = pl.pallas_call(
        first_kernel,
        out_shape=(
            shape((N_DOM, 24, 128), BF),
            shape((24, 128), BF),
            shape((BD, BW), F32),
            shape((K * BD, N_BLK * 32), BF),
            shape((K * BD, N_BLK * 16), BF),
            shape((K * BD, 64), jnp.int32),
        ),
        in_specs=[vmem] * 7,
        out_specs=[vmem] * 6,
        scratch_shapes=[pltpu.VMEM((128, 128), jnp.int32)],
        compiler_params=limit,
    )(scalars, z1, colidx.T, source, obj_weight.reshape(8, 128), offd, dinv)
    z2 = shift(spread(shift(message, "dom"), own, 48), "blk")
    perf = perf_block.shape[0]
    adjoint, sums = pl.pallas_call(
        last_kernel,
        out_shape=(shape((BD, BW), F32), shape((N_BLK, 128), F32)),
        in_specs=[vmem] * 10,
        out_specs=(vmem, vmem),
        compiler_params=limit,
    )(
        z2,
        *tables,
        forcing,
        perf_sens.T,
        perf_block.reshape(1, perf),
        perf_well.reshape(1, perf),
        offd,
        dinv,
    )
    terms = shift(sums.reshape(N_BLK, 1, 128), "blk")
    adjoint, control_grad = pl.pallas_call(
        result_kernel,
        out_shape=(shape((BD, BW), F32), shape((1, 8), F32)),
        in_specs=[vmem] * 2,
        out_specs=(vmem, vmem),
        compiler_params=small,
    )(terms, adjoint)
    return (adjoint, control_grad.reshape(8))


def solution(mesh):
    placed = (
        P(("dom", "blk"), None),
        P(("dom", "blk"), None),
        P(("dom", "blk"), None, None),
        P(None, ("dom", "blk")),
        P(("dom", "blk"), None),
        P("dom", None),
        P("dom"),
        P(("dom", "blk")),
        P(("dom", "blk")),
        P(("dom", "blk"), None),
        P(),
        P(),
    )
    return jax.shard_map(
        body,
        mesh=mesh,
        in_specs=placed,
        out_specs=(P(("dom", "blk"), None), P(("dom", "blk"))),
        check_vma=False,
    )
```

```python
import jax
import jax.numpy as jnp
from jax import lax
from jax.experimental import pallas as pl
from jax.experimental.pallas import tpu as pltpu
from jax.sharding import PartitionSpec as P

N_DOM = 32
N_BLK = 8
BD = 16
BW = 192
K = 6
PB = 128
FB = 64
GROUP = 4
BF = jnp.bfloat16
F32 = jnp.float32


def nt_dot(a, b):
    return lax.dot_general(a, b, (((1,), (1,)), ((), ())), preferred_element_type=F32)


def packed(rows):
    tails = jnp.concatenate([rows[0:8, 128:192], rows[8:16, 128:192]], axis=1)
    return jnp.concatenate([rows[:, 0:128], tails], axis=0)


def three_parts(x):
    high = x.astype(BF)
    rest = x - high.astype(F32)
    mid = rest.astype(BF)
    return high, mid, (rest - mid.astype(F32)).astype(BF)


def entry_kernel(lam_hbm, face_hbm, message_ref, own_ref, lam_ref, face_ref, sems):
    copies = [pltpu.make_async_copy(lam_hbm, lam_ref, sems.at[0]), pltpu.make_async_copy(face_hbm, face_ref, sems.at[1])]
    for copy in copies:
        copy.start()
    for copy in copies:
        copy.wait()
    own = packed(lam_ref[...].astype(F32))
    face = jnp.concatenate([face_ref[...].astype(F32), jnp.zeros((1, 64), F32)], axis=1)
    message = jnp.concatenate([own, jnp.broadcast_to(face, (8, 128))], axis=0).astype(BF)
    own_ref[...] = message
    for slot in range(N_DOM):
        message_ref[slot] = message


def first_select_kernel(scalars_ref, incoming_ref, own_ref, _, __, out_ref, face_ref):
    got = select_kernel(scalars_ref, incoming_ref, own_ref, out_ref)
    face_ref[...] = got[24:32]


def select_kernel(scalars_ref, incoming_ref, own_ref, out_ref):
    got = incoming_ref[jnp.max(scalars_ref[0:1, 0:1])].astype(F32)
    own = own_ref[...].astype(F32)
    rows = [own[0:16], got[0:16], own[16:24], got[16:24]]
    message = jnp.concatenate(rows, axis=0).astype(BF)
    for slot in range(N_BLK):
        out_ref[slot] = message
    return got


def second_select_kernel(scalars_ref, incoming_ref, own_ref, out_ref):
    select_kernel(scalars_ref, incoming_ref, own_ref, out_ref)


def prepare_kernel(
    partner_ref, step_ref, columns_hbm, source_hbm, weights_hbm, forcing_ref, cols_ref, scalars_ref, columns, source, weights, square, sems
):
    scalars_ref[...] = jnp.full((8, 128), partner_ref[0], jnp.int32)
    pairs = [(columns_hbm, columns), (source_hbm, source), (weights_hbm, weights)]
    copies = [pltpu.make_async_copy(*pair, sems.at[i]) for i, pair in enumerate(pairs)]
    for copy in copies:
        copy.start()
    for copy in copies:
        copy.wait()
    square[0:K, 0:BD] = columns[...]
    cols_ref[...] = square[...].T[0:BD, :]
    number = lax.broadcasted_iota(jnp.int32, (8, 128), 0) * 128 + lax.broadcasted_iota(jnp.int32, (8, 128), 1)
    weight = jnp.sum(jnp.where(number == step_ref[0], weights[...], 0.0), keepdims=True)
    forcing_ref[...] = source[...].astype(F32) * weight


def gather_tables(face, columns, main_ref, tail_ref, upper_ref):
    lane_face = lax.broadcasted_iota(jnp.int32, (BD, FB), 1)
    lane_main = lax.broadcasted_iota(jnp.int32, (BD, N_BLK * 32), 1)
    lane_tail = lax.broadcasted_iota(jnp.int32, (BD, N_BLK * 16), 1)
    for k in range(K):
        rows = slice(k * BD, (k + 1) * BD)
        c = columns[:, k : k + 1]
        seen = jnp.where(lane_face == c - PB, face, 0.0)
        halo = jnp.sum(seen, axis=1, keepdims=True).astype(jnp.int32)
        other = (c >= PB).astype(jnp.int32)
        block = jnp.where(c >= PB, halo, c)
        dev, row = block // BD, block % BD
        main_ref[rows, :] = jnp.where(lane_main == dev * 32 + other * 16 + row, 1.0, 0.0).astype(BF)
        tail_ref[rows, :] = jnp.where(lane_tail == dev * 16 + other * 8 + row % 8, 1.0, 0.0).astype(BF)
        upper_ref[rows, :] = jnp.broadcast_to(row // 8, (BD, 64))


def sweep(z_ref, main_ref, tail_ref, upper_ref, forcing, offd, dinv):
    main = z_ref[:, 0:32, :].reshape(N_BLK * 32, 128)
    tails = z_ref[:, 32:48, :].reshape(N_BLK * 16, 128)
    got_main = jnp.dot(main_ref[...], main, preferred_element_type=F32)
    got_tail = jnp.dot(tail_ref[...], tails, preferred_element_type=F32)
    got_tail = jnp.where(upper_ref[...] > 0, got_tail[:, 64:128], got_tail[:, 0:64])
    width = GROUP * BW
    forcing = jnp.concatenate([forcing] * GROUP, axis=1)
    row_id = lax.broadcasted_iota(jnp.int32, (BD, width), 0)
    part = lax.broadcasted_iota(jnp.int32, (BD, width), 1) // BW
    pieces = []
    for pair in range(K // 2):
        first, second = (slice(k * BD, (k + 1) * BD) for k in (2 * pair, 2 * pair + 1))
        pieces.append(got_main[first])
        pieces.append(jnp.concatenate([got_tail[first], got_main[second][:, 0:64]], axis=1))
        pieces.append(jnp.concatenate([got_main[second][:, 64:128], got_tail[second]], axis=1))
    ones = jnp.ones((BD, 128), BF)
    total = jnp.zeros((BD, BW), F32)
    for first in range(0, BD, GROUP):
        coupled = []
        for block in range(first, first + GROUP):
            factors = [jnp.broadcast_to(piece[block : block + 1, :], (16, 128)) for piece in pieces]
            lanes = []
            for row in range(0, BW, 16):
                partial = None
                for tile, factor in enumerate(factors):
                    term = offd[block, row : row + 16, tile * 128 : (tile + 1) * 128].astype(F32) * factor
                    partial = term if partial is None else partial + term
                lanes.append(partial)
            lanes = jnp.concatenate(lanes, axis=0)
            high = lanes.astype(BF)
            coupled.append(nt_dot(ones, high) + nt_dot(ones, (lanes - high.astype(F32)).astype(BF)))
        coupled = jnp.concatenate(coupled, axis=1)
        rhs = jnp.where(row_id == part + first, forcing - coupled, 0.0).astype(BF)
        total = total + nt_dot(rhs, dinv[:, first * BW : (first + GROUP) * BW])
    return total


def first_kernel(
    face_ref,
    z_ref,
    cols_ref,
    forcing_ref,
    offd,
    dinv,
    out_ref,
    own_ref,
    main_ref,
    tail_ref,
    upper_ref,
):
    gather_tables(face_ref[0:1, 0:FB], cols_ref[...], main_ref, tail_ref, upper_ref)
    forcing = forcing_ref[...]
    total = sweep(z_ref, main_ref, tail_ref, upper_ref, forcing, offd, dinv)
    message = packed(total).astype(BF)
    own_ref[...] = message
    for slot in range(N_DOM):
        out_ref[slot] = message


def last_kernel(
    z_ref, main_ref, tail_ref, upper_ref, forcing_ref, sens_ref, block_ref, well_ref, offd, dinv, adj_ref, sum_ref
):
    total = sweep(z_ref, main_ref, tail_ref, upper_ref, forcing_ref[...], offd, dinv)
    adj_ref[...] = total
    sens = sens_ref[...]
    dots = sum(jnp.dot(part, sens, preferred_element_type=F32) for part in three_parts(total))
    perf = dots.shape[1]
    row_id = lax.broadcasted_iota(jnp.int32, (BD, perf), 0)
    contrib = jnp.sum(jnp.where(row_id == block_ref[...], dots, 0.0), axis=0, keepdims=True)
    well = well_ref[...]
    target = lax.broadcasted_iota(jnp.int32, (N_BLK, perf), 0)
    spread = jnp.where(target == well // 8, -contrib, 0.0)
    lane = lax.broadcasted_iota(jnp.int32, (128, perf), 0)
    hot = jnp.where(lane == well % 8, 1.0, 0.0).astype(BF)
    sum_ref[...] = sum(nt_dot(part, hot) for part in three_parts(spread))


def shift(message, axis):
    return lax.all_to_all(message, axis, split_axis=0, concat_axis=0, tiled=True)


def result_kernel(terms_ref, total_ref, adj_ref, grad_ref):
    adj_ref[...] = total_ref[...]
    terms = terms_ref[:, 0, :]
    grad_ref[...] = jnp.sum(terms, axis=0, keepdims=True)[:, 0:8]


def in_hbm(x):
    return pltpu.with_memory_space_constraint(x, pltpu.HBM)


def body(
    source,
    lam_init,
    offd,
    dinv,
    colidx,
    face_list,
    partner,
    perf_block,
    perf_well,
    perf_sens,
    obj_weight,
    step_index,
):
    vmem = pl.BlockSpec(memory_space=pltpu.VMEM)
    smem = pl.BlockSpec(memory_space=pltpu.SMEM)
    hbm = pl.BlockSpec(memory_space=pltpu.HBM)

    def shape(dims, dtype):
        return jax.ShapeDtypeStruct(dims, dtype)

    limit = pltpu.CompilerParams(vmem_limit_bytes=4 * 1024 * 1024)
    small = pltpu.CompilerParams(vmem_limit_bytes=4 * 1024 * 1024)
    message, own = pl.pallas_call(
        entry_kernel,
        out_shape=(shape((N_DOM, 32, 128), BF), shape((32, 128), BF)),
        in_specs=[hbm] * 2,
        out_specs=[vmem] * 2,
        scratch_shapes=[pltpu.VMEM((BD, BW), BF), pltpu.VMEM((1, FB), jnp.int32), pltpu.SemaphoreType.DMA((2,))],
        compiler_params=small,
    )(in_hbm(lam_init), in_hbm(face_list))
    forcing, cols, scalars = pl.pallas_call(
        prepare_kernel,
        out_shape=(shape((BD, BW), F32), shape((BD, 128), jnp.int32), shape((8, 128), jnp.int32)),
        in_specs=[smem] * 2 + [hbm] * 3,
        out_specs=[vmem] * 3,
        scratch_shapes=[
            pltpu.VMEM((K, BD), jnp.int32),
            pltpu.VMEM((BD, BW), BF),
            pltpu.VMEM((8, 128), F32),
            pltpu.VMEM((128, 128), jnp.int32),
            pltpu.SemaphoreType.DMA((3,)),
        ],
        compiler_params=small,
    )(partner, step_index, in_hbm(colidx.T), in_hbm(source), in_hbm(obj_weight.reshape(8, 128)))
    z1, face = pl.pallas_call(
        first_select_kernel,
        out_shape=(shape((N_BLK, 48, 128), BF), shape((8, 128), F32)),
        in_specs=[vmem] * 3 + [hbm] * 2,
        out_specs=[vmem] * 2,
        compiler_params=small,
    )(scalars, shift(message, "dom"), own, in_hbm(offd), in_hbm(dinv))
    z1 = shift(z1, "blk")
    message, own, *tables = pl.pallas_call(
        first_kernel,
        out_shape=(
            shape((N_DOM, 24, 128), BF),
            shape((24, 128), BF),
            shape((K * BD, N_BLK * 32), BF),
            shape((K * BD, N_BLK * 16), BF),
            shape((K * BD, 64), jnp.int32),
        ),
        in_specs=[vmem] * 6,
        out_specs=[vmem] * 5,
        compiler_params=limit,
    )(face, z1, cols, forcing, offd, dinv)
    z2 = pl.pallas_call(
        second_select_kernel,
        out_shape=shape((N_BLK, 48, 128), BF),
        in_specs=[vmem] * 3,
        out_specs=vmem,
        compiler_params=small,
    )(scalars, shift(message, "dom"), own)
    z2 = shift(z2, "blk")
    perf = perf_block.shape[0]
    adjoint, sums = pl.pallas_call(
        last_kernel,
        out_shape=(shape((BD, BW), F32), shape((N_BLK, 128), F32)),
        in_specs=[vmem] * 10,
        out_specs=(vmem, vmem),
        compiler_params=limit,
    )(
        z2,
        *tables,
        forcing,
        perf_sens.T,
        perf_block.reshape(1, perf),
        perf_well.reshape(1, perf),
        offd,
        dinv,
    )
    terms = shift(sums.reshape(N_BLK, 1, 128), "blk")
    adjoint, control_grad = pl.pallas_call(
        result_kernel,
        out_shape=(shape((BD, BW), F32), shape((1, 8), F32)),
        in_specs=[vmem] * 2,
        out_specs=(vmem, vmem),
        compiler_params=small,
    )(terms, adjoint)
    return (adjoint, control_grad.reshape(8))


def solution(mesh):
    placed = (
        P(("dom", "blk"), None),
        P(("dom", "blk"), None),
        P(("dom", "blk"), None, None),
        P(None, ("dom", "blk")),
        P(("dom", "blk"), None),
        P("dom", None),
        P("dom"),
        P(("dom", "blk")),
        P(("dom", "blk")),
        P(("dom", "blk"), None),
        P(),
        P(),
    )
    return jax.shard_map(
        body,
        mesh=mesh,
        in_specs=placed,
        out_specs=(P(("dom", "blk"), None), P(("dom", "blk"))),
        check_vma=False,
    )
```
